256 devices in a mesh: alpha: 16 (over x, z_lo), beta: 8 (over y, core), ints: 2 (over z_hi).
Axes of the slice: x: 4, y: 4, z: 8 (z_hi: 2, z_lo: 4; z = z_hi * 4 + z_lo), core: 2. Of those that a mesh axis runs over, the one named last changes fastest.
Arguments:
- ci_vector: float32 [4096, 4096], P('beta', 'alpha'), may hold values from -6 to 6
- integrals: float32 [32, 32], P('ints'), may hold values from -1 to 1
- alpha_source: int32 [32, 4096], P('ints', 'alpha'), may hold values from 0 to 4095
- alpha_sign: int32 [32, 4096], P('ints', 'alpha'), may hold values from -1 to 1
- beta_tiles: int32 [32, 32], replicated, may hold values from 0 to 31, each once within a row
- beta_offsets: int32 [32, 32, 128], replicated, may hold values from 0 to 127, each once within a row
- beta_sign: int32 [32, 4096], replicated, may hold values from -1 to 1
Outputs:
- sigma: float32 [4096, 4096], P('beta', 'alpha')
The draws below stay inside these ranges and needn't reach their ends.
Inputs may be any that keep to these rules, and one draw needn't show every extreme that they name: Each row of beta_tiles names every tile once. Each row of beta_offsets names every position of a tile once.
All inputs are finite; a program needn't handle non-finite values.
Results may differ from the reference program's by a relative error of at most 0.00007.
Values sent between devices are 32-bit elements; how exact they have to be, the bound alone decides.
No kernel may reach another device: no remote copies, remote signals or barrier semaphores. Data moves between devices by JAX's collectives and lax.ppermute only.
A program may use at most 128 MiB of HBM per device.

```python
import jax
import jax.numpy as jnp
from jax import lax

P_SIZE = 32
TILE = 128
RA = 256
NA = 4096
NB = 4096
NTB = 32


def touch_ends(result, own_key, least, largest):
    extent = result.shape
    spot = [jax.random.randint(jax.random.fold_in(own_key, axis), (), 0, extent[axis]) for axis in range(len(extent))]
    result = result.at[tuple(spot)].set(least)
    longest = extent.index(max(extent))
    spot[longest] = (spot[longest] + 1) % extent[longest]
    return result.at[tuple(spot)].set(largest)


def levels(own_key, extent, pieces, low, largest):
    level, own = 1.0, jax.random.fold_in(own_key, 6)
    for axis_at, parts in pieces:
        steps = jnp.exp(jax.random.uniform(jax.random.fold_in(own, axis_at), (parts,), jnp.float32, low / len(pieces), largest / len(pieces)))
        level = level * jnp.repeat(steps, extent[axis_at] // parts).reshape([-1 if axis == axis_at else 1 for axis in range(len(extent))])
    return level


def noise(own_key, extent, spread, most, shards=(), kind=jnp.bfloat16):
    values = jax.random.normal(own_key, extent, jnp.float32) * spread
    if len(shards) > 0:
        values = levels(own_key, extent, shards, -0.22, 0.18) * values
    return jnp.clip(values, min=-most, max=most).astype(kind)


def setup_inputs(seed: int = 0) -> dict:
    seeds = jax.random.split(jax.random.key(seed), 8)
    return {
        "ci_vector": noise(seeds[0], (NB, NA), 1.0, 6.0, ((0, 8), (1, 16)), jnp.float32),
        "integrals": noise(seeds[1], (P_SIZE, P_SIZE), P_SIZE ** -0.5, 1.0, ((0, 2),), jnp.float32),
        "alpha_source": touch_ends(jax.random.randint(seeds[2], (P_SIZE, NA), 0, NA), jax.random.fold_in(seeds[2], 1), 0, NA - 1).astype(jnp.int32),
        "alpha_sign": touch_ends(jax.random.randint(seeds[3], (P_SIZE, NA), -1, 2), jax.random.fold_in(seeds[3], 1), -1, 1).astype(jnp.int32),
        "beta_tiles": jax.vmap(lambda own: jax.random.permutation(own, NTB))(jax.random.split(seeds[4], P_SIZE)).reshape((P_SIZE, NTB)).astype(jnp.int32),
        "beta_offsets": jax.vmap(lambda own: jax.random.permutation(own, TILE))(jax.random.split(seeds[5], P_SIZE * NTB)).reshape((P_SIZE, NTB, TILE)).astype(jnp.int32),
        "beta_sign": touch_ends(jax.random.randint(seeds[6], (P_SIZE, NB), -1, 2), jax.random.fold_in(seeds[6], 1), -1, 1).astype(jnp.int32),
    }


def reference(ci_vector, integrals, alpha_source, alpha_sign, beta_tiles, beta_offsets, beta_sign):
    source = (beta_tiles[:, :, None] * TILE + beta_offsets).reshape(P_SIZE, NB).astype(jnp.int32)
    bsign = beta_sign.astype(jnp.float32)
    blocks_src = alpha_source.reshape(P_SIZE, NA // RA, RA).transpose(1, 0, 2)
    blocks_sign = alpha_sign.astype(jnp.float32).reshape(P_SIZE, NA // RA, RA).transpose(1, 0, 2)

    def one_block(pair):
        idx, sgn = pair
        excited = jnp.take(ci_vector, idx, axis=1)
        excited = jnp.moveaxis(excited, 1, 0) * sgn[:, None, :]
        mixed = jnp.einsum('kl,kba->lba', integrals, excited, precision=lax.Precision.HIGHEST)
        pulled = jnp.take_along_axis(mixed, source[:, :, None], axis=1)
        return jnp.sum(pulled * bsign[:, :, None], axis=0)

    out = lax.map(one_block, (blocks_src, blocks_sign))
    return jnp.moveaxis(out, 0, 1).reshape(NB, NA)
```

```python
import functools

import jax
import jax.numpy as jnp
from jax import lax
from jax.experimental import pallas as pl
from jax.experimental.pallas import tpu as pltpu
from jax.sharding import PartitionSpec as P

LANES = 128
GROUP = 8
RING = 4
AXES = ("alpha", "ints")


def chip(x, z, ints):
    run = RING
    full = run * ints
    x, z = x % RING, z % full
    return (x * run + z % run) * ints + z // run


def shift(value, dx, dz):
    ints = lax.axis_size("ints")
    rows = lax.axis_size("alpha") // RING
    pairs = [
        (chip(x, z, ints), chip(x + dx, z + dz, ints))
        for x in range(rows)
        for z in range(RING * ints)
    ]
    return lax.ppermute(value, AXES, pairs)


def spread(block, first, second):
    n = block.shape[0]
    half = n // 2
    ahead = shift(block, *[-s for s in first])
    behind = shift(block, *first)
    over_a = shift(ahead[:half], *[-s for s in first])
    over_b = shift(behind[half:], *first)
    line = jnp.concatenate([block, ahead, behind, over_a, over_b], 0)
    next_ahead = shift(line, *[-s for s in second])
    next_behind = shift(line, *second)
    last_a = shift(next_ahead[: 2 * n], *[-s for s in second])
    last_b = shift(next_behind[2 * n :], *second)
    pieces = []
    for step, array, lo, hi in (
        (0, line, 0, 4),
        (1, next_ahead, 0, 4),
        (3, next_behind, 0, 4),
        (2, last_a, 0, 2),
        (2, last_b, 2, 4),
    ):
        for at in range(lo, hi):
            along = (0, 1, 3, 2)[at]
            place = (first[0] * along + second[0] * step, first[1] * along + second[1] * step)
            pieces.append((place, array, (at - lo) * n))
    return pieces


def kernel(copies, steps, pairs, slots, *refs):
    arrays = refs[: len({c[0] for c in copies})]
    base_ref, src_ref, tgt_ref, sign_ref, vb_ref, off_ref, bs_ref, out_ref = refs[len(arrays) : len(arrays) + 8]
    table, g_ref, y_ref, vhi_ref, vlo_ref, sems = refs[len(arrays) + 8 :]
    dmas = []
    for n, (which, start, rows, slot, inner) in enumerate(copies):
        dmas.append(
            pltpu.make_async_copy(
                arrays[which].at[pl.ds(start, rows)],
                table.at[pl.ds(base_ref[slot] + inner, rows)],
                sems.at[n],
            )
        )
    for dma in dmas:
        dma.start()
    v = vb_ref[...]
    high = v.astype(jnp.bfloat16)
    vhi_ref[...] = high
    vlo_ref[...] = (v - high.astype(jnp.float32)).astype(jnp.bfloat16)
    out_ref[...] = jnp.zeros_like(out_ref)
    for dma in dmas:
        dma.wait()

    rows = GROUP * pairs
    quads = slots

    def mix(step, carry):
        for r in range(rows):
            g_ref[r] = table[src_ref[step * rows + r]]
        flat = g_ref.reshape(rows * quads, LANES)
        sign = sign_ref[pl.ds(step, 1), :].astype(jnp.bfloat16)
        left_hi = vhi_ref[...] * sign
        left_lo = vlo_ref[...] * sign
        for q in range(quads):
            g = flat[pl.ds(q, rows, stride=quads), :]
            hi = g.astype(jnp.bfloat16)
            lo = (g - hi.astype(jnp.float32)).astype(jnp.bfloat16)
            got = (
                jnp.dot(left_hi, hi, preferred_element_type=jnp.float32)
                + jnp.dot(left_hi, lo, preferred_element_type=jnp.float32)
                + jnp.dot(left_lo, hi, preferred_element_type=jnp.float32)
            )
            y_ref[:, q, pl.ds(step * GROUP, GROUP), :] = got.reshape(pairs, GROUP, LANES)
        return carry

    lax.fori_loop(0, steps, mix, 0)
    tiles = out_ref.shape[0]
    lines = lax.broadcasted_iota(jnp.int32, (LANES, LANES), 0)

    def place(pair, carry):
        for q in range(quads):
            t = tgt_ref[pair * quads + q]
            off = off_ref[pl.ds(pair * tiles + t, 1), :]
            sgn = bs_ref[pl.ds(pair * tiles + t, 1), :]
            hot = jnp.where(lines == off, sgn, 0.0).astype(jnp.bfloat16)
            y = y_ref[pair, q]
            hi = y.astype(jnp.bfloat16)
            lo = (y - hi.astype(jnp.float32)).astype(jnp.bfloat16)
            got = jnp.dot(hi, hot, preferred_element_type=jnp.float32) + jnp.dot(
                lo, hot, preferred_element_type=jnp.float32
            )
            out_ref[t] += got
        return carry

    lax.fori_loop(0, pairs, place, 0)


def local(ci_vector, integrals, alpha_source, alpha_sign, beta_tiles, beta_offsets, beta_sign):
    rows_b, cols_a = ci_vector.shape
    pairs, tiles, tile = beta_offsets.shape
    slots = rows_b // tile
    ints = lax.axis_size("ints")
    mine = lax.axis_index("ints")
    cols = cols_a // ints
    alpha = lax.axis_index("alpha")
    x, z = alpha // RING, alpha % RING

    swap = [(0, 1), (1, 0)]
    both = jnp.stack([alpha_source, alpha_sign])
    keep = lax.dynamic_slice_in_dim(both, mine * cols, cols, 2)
    give = lax.dynamic_slice_in_dim(both, (1 - mine) * cols, cols, 2)
    got = lax.ppermute(give, "ints", swap)
    v_got = lax.ppermute(integrals, "ints", swap)
    first = mine == 0
    full = jnp.concatenate([jnp.where(first, keep, got), jnp.where(first, got, keep)], 1)
    v = jnp.concatenate([jnp.where(first, integrals, v_got), jnp.where(first, v_got, integrals)], 0)
    flat = full.transpose(0, 2, 1).reshape(2, cols * pairs)
    source = flat[0]
    steps = cols // GROUP
    sign = flat[1].reshape(steps, GROUP * pairs).astype(jnp.float32)
    eye = jnp.eye(GROUP, dtype=jnp.float32)
    vb = (v.T[:, None, None, :] * eye[None, :, :, None]).reshape(pairs * GROUP, GROUP * pairs)

    my_first = lax.axis_index("beta") * slots
    wanted = my_first + jnp.arange(slots, dtype=jnp.int32)
    hit = beta_tiles[:, :, None] == wanted[None, None, :]
    target = jnp.sum(jnp.where(hit, jnp.arange(tiles, dtype=jnp.int32)[None, :, None], 0), axis=1).reshape(-1)

    columns = ci_vector.T.reshape(cols_a, slots, tile)
    n = cols_a // 2
    pieces_a = spread(columns[:n], (0, 1), (1, 0))
    pieces_b = spread(columns[n:], (1, 0), (0, 1))
    arrays, copies = [], []
    for inner, pieces in ((0, pieces_a), (n, pieces_b)):
        for (dx, dz), array, start in pieces:
            if not any(array is a for a in arrays):
                arrays.append(array)
            which = next(i for i, a in enumerate(arrays) if a is array)
            copies.append((which, start, n, (dx % RING) * RING + dz % RING, inner))
    d = jnp.arange(RING * RING, dtype=jnp.int32)
    base = (((x + d // RING) % RING) * RING + (z + d % RING) % RING) * cols_a

    smem = pl.BlockSpec(memory_space=pltpu.SMEM)
    vmem = pl.BlockSpec(memory_space=pltpu.VMEM)
    partial = pl.pallas_call(
        functools.partial(kernel, tuple(copies), steps, pairs, slots),
        out_shape=jax.ShapeDtypeStruct((tiles, cols, tile), jnp.float32),
        in_specs=[pl.BlockSpec(memory_space=pl.ANY)] * len(arrays) + [smem] * 3 + [vmem] * 4,
        out_specs=vmem,
        scratch_shapes=[
            pltpu.VMEM((lax.axis_size("alpha") * cols_a, slots, tile), jnp.float32),
            pltpu.VMEM((GROUP * pairs, slots, tile), jnp.float32),
            pltpu.VMEM((pairs, slots, cols, tile), jnp.float32),
            pltpu.VMEM((GROUP * pairs, GROUP * pairs), jnp.bfloat16),
            pltpu.VMEM((GROUP * pairs, GROUP * pairs), jnp.bfloat16),
            pltpu.SemaphoreType.DMA((len(copies),)),
        ],
        compiler_params=pltpu.CompilerParams(vmem_limit_bytes=40 * 1024 * 1024),
        name="sigma_partial",
    )(
        *arrays,
        base,
        source,
        target,
        sign,
        vb,
        beta_offsets.reshape(pairs * tiles, tile),
        beta_sign.astype(jnp.float32).reshape(pairs * tiles, tile),
    )
    summed = lax.psum_scatter(partial, "beta", scatter_dimension=0, tiled=True)
    other = lax.ppermute(summed, "ints", swap)
    left = jnp.where(first, summed, other)
    right = jnp.where(first, other, summed)
    joined = jnp.concatenate([left, right], 1)
    return joined.transpose(0, 2, 1).reshape(rows_b, cols_a)


def solution(mesh):
    return jax.shard_map(
        local,
        mesh=mesh,
        in_specs=(
            P("beta", "alpha"),
            P("ints", None),
            P("ints", "alpha"),
            P("ints", "alpha"),
            P(),
            P(),
            P(),
        ),
        out_specs=P("beta", "alpha"),
        check_vma=False,
    )
```

```python
import functools

import jax
import jax.numpy as jnp
from jax import lax
from jax.experimental import pallas as pl
from jax.experimental.pallas import tpu as pltpu
from jax.sharding import PartitionSpec as P

LANES = 128
GROUP = 8
RING = 4
CORES = 2
AXES = ("alpha", "ints")


def chip(x, z, ints):
    run = RING
    full = run * ints
    x, z = x % RING, z % full
    return (x * run + z % run) * ints + z // run


def shift(value, dx, dz):
    ints = lax.axis_size("ints")
    rows = lax.axis_size("alpha") // RING
    pairs = [
        (chip(x, z, ints), chip(x + dx, z + dz, ints))
        for x in range(rows)
        for z in range(RING * ints)
    ]
    return lax.ppermute(value, AXES, pairs)


def spread(block, first, second):
    n = block.shape[0]
    fore = lambda value, axis: shift(value, *[-s for s in axis])
    back = lambda value, axis: shift(value, *axis)
    ahead = fore(block, first)
    behind = back(block, first)
    early = jnp.concatenate([block, ahead], 0)
    over = fore(ahead, first)
    late = jnp.concatenate([behind, over], 0)
    early_ahead, early_behind = fore(early, second), back(early, second)
    late_ahead, late_behind = fore(late, second), back(late, second)
    early_over = fore(early_ahead, second)
    late_over = back(late_behind, second)
    pieces = []
    for step, array, steps in (
        (0, (block,), (0,)),
        (0, (ahead,), (1,)),
        (0, (behind,), (3,)),
        (0, (over,), (2,)),
        (1, early_ahead, (0, 1)),
        (3, early_behind, (0, 1)),
        (1, late_ahead, (3, 2)),
        (3, late_behind, (3, 2)),
        (2, early_over, (0, 1)),
        (2, late_over, (3, 2)),
    ):
        array = array[0] if isinstance(array, tuple) else array
        for at, along in enumerate(steps):
            place = (first[0] * along + second[0] * step, first[1] * along + second[1] * step)
            pieces.append((place, array, at * n))
    return pieces


def kernel(copies, steps, pairs, slots, *refs):
    arrays = refs[: len({c[0] for c in copies})]
    base_ref, src_ref, tgt_ref, sign_ref, vb_ref, off_hbm, bs_hbm, keep_hbm, give_hbm = refs[
        len(arrays) : len(arrays) + 9
    ]
    table, g_ref, y_ref, vhi_ref, vlo_ref, off_ref, bs_ref, acc_ref, sems, sem_off, sem_bs, sem_out = refs[
        len(arrays) + 9 :
    ]
    dmas = []
    for n, (which, start, rows, slot, inner) in enumerate(copies):
        dmas.append(
            pltpu.make_async_copy(
                arrays[which].at[pl.ds(start, rows)],
                table.at[pl.ds(base_ref[slot] + inner, rows)],
                sems.at[n],
            )
        )
    for dma in dmas:
        dma.start()
    load_off = pltpu.make_async_copy(off_hbm, off_ref, sem_off)
    load_bs = pltpu.make_async_copy(bs_hbm, bs_ref, sem_bs)
    load_off.start()
    load_bs.start()
    v = vb_ref[...]
    high = v.astype(jnp.bfloat16)
    vhi_ref[...] = high
    vlo_ref[...] = (v - high.astype(jnp.float32)).astype(jnp.bfloat16)
    acc_ref[...] = jnp.zeros_like(acc_ref)
    for dma in dmas:
        dma.wait()

    rows = GROUP * pairs

    def fetch(step, buffer):
        for r in range(rows):
            g_ref[buffer, r] = table[src_ref[step * rows + r]]

    def mix(step, buffer):
        flat = g_ref.at[buffer].reshape(rows * slots, LANES)
        sign = sign_ref[pl.ds(step, 1), :].astype(jnp.bfloat16)
        left_hi = vhi_ref[...] * sign
        left_lo = vlo_ref[...] * sign
        g = jnp.concatenate([flat[pl.ds(q, rows, stride=slots), :] for q in range(slots)], 1)
        hi = g.astype(jnp.bfloat16)
        lo = (g - hi.astype(jnp.float32)).astype(jnp.bfloat16)
        got = (
            jnp.dot(left_hi, hi, preferred_element_type=jnp.float32)
            + jnp.dot(left_hi, lo, preferred_element_type=jnp.float32)
            + jnp.dot(left_lo, hi, preferred_element_type=jnp.float32)
        )
        for q in range(slots):
            part = got[:, q * LANES : (q + 1) * LANES]
            y_ref[:, q, pl.ds(step * GROUP, GROUP), :] = part.reshape(pairs, GROUP, LANES)

    fetch(0, 0)

    def two(half, carry):
        step = half * 2
        fetch(step + 1, 1)
        mix(step, 0)
        fetch(jnp.minimum(step + 2, steps - 1), 0)
        mix(step + 1, 1)
        return carry

    lax.fori_loop(0, steps // 2, two, 0)
    load_off.wait()
    load_bs.wait()
    lines = lax.broadcasted_iota(jnp.int32, (LANES, LANES), 0)
    tiles = acc_ref.shape[0]

    def place(pair):
        found = []
        for q in range(slots):
            t = tgt_ref[pair * slots + q]
            spot = tgt_ref[(pairs + pair) * slots + q]
            off = off_ref[pl.ds(pair * tiles + t, 1), :]
            sgn = bs_ref[pl.ds(pair * tiles + t, 1), :].astype(jnp.float32)
            hot = jnp.where(lines == off, sgn, 0.0).astype(jnp.bfloat16)
            y = y_ref[pair, q]
            hi = y.astype(jnp.bfloat16)
            lo = (y - hi.astype(jnp.float32)).astype(jnp.bfloat16)
            left = jnp.concatenate([hi, lo], 1)
            right = jnp.concatenate([hot, hot], 0)
            found.append((spot, jnp.dot(left, right, preferred_element_type=jnp.float32)))
        for spot, value in found:
            acc_ref[spot] += value

    def two_pairs(half, carry):
        place(half * 2)
        place(half * 2 + 1)
        return carry

    lax.fori_loop(0, pairs // 2, two_pairs, 0)
    half = tiles // 2
    store_give = pltpu.make_async_copy(acc_ref.at[pl.ds(half, half)], give_hbm, sem_out.at[0])
    store_keep = pltpu.make_async_copy(acc_ref.at[pl.ds(0, half)], keep_hbm, sem_out.at[1])
    store_give.start()
    store_keep.start()
    store_give.wait()
    store_keep.wait()


def local(ci_vector, integrals, alpha_source, alpha_sign, beta_tiles, beta_offsets, beta_sign):
    rows_b, cols_a = ci_vector.shape
    pairs, tiles, tile = beta_offsets.shape
    slots = rows_b // tile
    ints = lax.axis_size("ints")
    mine = lax.axis_index("ints")
    cols = cols_a // ints
    alpha = lax.axis_index("alpha")
    x, z = alpha // RING, alpha % RING

    swap = [(0, 1), (1, 0)]
    both = jnp.stack([alpha_source, alpha_sign])
    keep = lax.dynamic_slice_in_dim(both, mine * cols, cols, 2)
    give = lax.dynamic_slice_in_dim(both, (1 - mine) * cols, cols, 2)
    got = lax.ppermute(give, "ints", swap)
    v_got = lax.ppermute(integrals, "ints", swap)
    first = mine == 0
    full = jnp.concatenate([jnp.where(first, keep, got), jnp.where(first, got, keep)], 1)
    v = jnp.concatenate([jnp.where(first, integrals, v_got), jnp.where(first, v_got, integrals)], 0)
    flat = full.transpose(0, 2, 1).reshape(2, cols * pairs)
    source = flat[0]
    steps = cols // GROUP
    sign = flat[1].reshape(steps, GROUP * pairs).astype(jnp.float32)
    eye = jnp.eye(GROUP, dtype=jnp.float32)
    vb = (v.T[:, None, None, :] * eye[None, :, :, None]).reshape(pairs * GROUP, GROUP * pairs)

    beta = lax.axis_index("beta")
    betas = lax.axis_size("beta")
    rings = betas // CORES
    y, core = beta // CORES, beta % CORES
    wanted = beta * slots + jnp.arange(slots, dtype=jnp.int32)
    hit = beta_tiles[:, :, None] == wanted[None, None, :]
    target = jnp.sum(jnp.where(hit, jnp.arange(tiles, dtype=jnp.int32)[None, :, None], 0), axis=1).reshape(-1)
    owner = target // slots
    away = (owner // CORES - y) % rings
    spot = ((owner % CORES) ^ core) * (tiles // CORES) + away * slots + target % slots
    target = jnp.concatenate([target, spot])

    columns = ci_vector.T.reshape(cols_a, slots, tile)
    n = cols_a // 2
    pieces_a = spread(columns[:n], (0, 1), (1, 0))
    pieces_b = spread(columns[n:], (1, 0), (0, 1))
    arrays, copies = [], []
    for inner, pieces in ((0, pieces_a), (n, pieces_b)):
        for (dx, dz), array, start in pieces:
            if not any(array is a for a in arrays):
                arrays.append(array)
            which = next(i for i, a in enumerate(arrays) if a is array)
            copies.append((which, start, n, (dx % RING) * RING + dz % RING, inner))
    d = jnp.arange(RING * RING, dtype=jnp.int32)
    base = (((x + d // RING) % RING) * RING + (z + d % RING) % RING) * cols_a

    smem = pl.BlockSpec(memory_space=pltpu.SMEM)
    vmem = pl.BlockSpec(memory_space=pltpu.VMEM)
    hbm = pl.BlockSpec(memory_space=pl.ANY)
    half = jax.ShapeDtypeStruct((tiles // CORES, cols, tile), jnp.float32)
    keep, give = pl.pallas_call(
        functools.partial(kernel, tuple(copies), steps, pairs, slots),
        out_shape=(half, half),
        in_specs=[hbm] * len(arrays) + [smem] * 3 + [vmem] * 2 + [hbm] * 2,
        out_specs=(hbm, hbm),
        scratch_shapes=[
            pltpu.VMEM((lax.axis_size("alpha") * cols_a, slots, tile), jnp.float32),
            pltpu.VMEM((2, GROUP * pairs, slots, tile), jnp.float32),
            pltpu.VMEM((pairs, slots, cols, tile), jnp.float32),
            pltpu.VMEM((GROUP * pairs, GROUP * pairs), jnp.bfloat16),
            pltpu.VMEM((GROUP * pairs, GROUP * pairs), jnp.bfloat16),
            pltpu.VMEM((pairs * tiles, tile), jnp.int32),
            pltpu.VMEM((pairs * tiles, tile), jnp.int32),
            pltpu.VMEM((tiles, cols, tile), jnp.float32),
            pltpu.SemaphoreType.DMA((len(copies),)),
            pltpu.SemaphoreType.DMA,
            pltpu.SemaphoreType.DMA,
            pltpu.SemaphoreType.DMA((2,)),
        ],
        compiler_params=pltpu.CompilerParams(vmem_limit_bytes=40 * 1024 * 1024),
        name="sigma_partial",
    )(
        *arrays,
        base,
        source,
        target,
        sign,
        vb,
        beta_offsets.reshape(pairs * tiles, tile),
        beta_sign.reshape(pairs * tiles, tile),
    )
    across = [(b, b ^ 1) for b in range(betas)]
    came = lax.ppermute(give, "beta", across)
    total = keep[:slots] + came[:slots]
    for far in (2, 1, 3):
        pairs_y = [(b, (b + far * CORES) % betas) for b in range(betas)]
        part = keep[far * slots : (far + 1) * slots] + came[far * slots : (far + 1) * slots]
        total = total + lax.ppermute(part, "beta", pairs_y)
    summed = total.transpose(0, 2, 1).reshape(rows_b, cols)
    other = lax.ppermute(summed, "ints", swap)
    return jnp.concatenate([jnp.where(first, summed, other), jnp.where(first, other, summed)], 1)


def solution(mesh):
    return jax.shard_map(
        local,
        mesh=mesh,
        in_specs=(
            P("beta", "alpha"),
            P("ints", None),
            P("ints", "alpha"),
            P("ints", "alpha"),
            P(),
            P(),
            P(),
        ),
        out_specs=P("beta", "alpha"),
        check_vma=False,
    )
```

```python
import functools

import jax
import jax.numpy as jnp
from jax import lax
from jax.experimental import pallas as pl
from jax.experimental.pallas import tpu as pltpu
from jax.sharding import PartitionSpec as P

LANES = 128
GROUP = 8
RING = 4
CORES = 2
CHUNKS = 2
UNROLL = 4
FLIGHT = 5
AXES = ("alpha", "beta", "ints")


def device(x, z, y, core):
    ints = lax.axis_size("ints")
    x, z = x % RING, z % (RING * ints)
    alpha = x * RING + z % RING
    return (alpha * lax.axis_size("beta") + y * CORES + core) * ints + z // RING


def move(value, axis, step):
    pairs = []
    for x in range(lax.axis_size("alpha") // RING):
        for z in range(RING * lax.axis_size("ints")):
            for y in range(lax.axis_size("beta") // CORES):
                for core in range(CORES):
                    dx, dz = (step, 0) if axis != core else (0, step)
                    pairs.append((device(x, z, y, core), device(x + dx, z + dz, y, core)))
    return lax.ppermute(value, AXES, pairs)


def spread(block, packet):
    held = {"own": block}
    order = []

    def send(name, source, axis, step):
        value = held[source]
        if len(order) >= FLIGHT:
            value, _ = lax.optimization_barrier((value, held[order[-FLIGHT]]))
        held[name] = move(value, axis, step)
        order.append(name)

    send("ahead", "own", 0, -1)
    send("behind", "own", 0, 1)
    send("own_ahead", "own", 1, -1)
    send("own_behind", "own", 1, 1)
    send("over", "ahead", 0, -1)
    send("behind_behind", "behind", 1, 1)
    send("ahead_ahead", "ahead", 1, -1)
    send("ahead_behind", "ahead", 1, 1)
    send("behind_ahead", "behind", 1, -1)
    packet, _ = lax.optimization_barrier((packet, held[order[-FLIGHT]]))
    held["packet"] = lax.ppermute(packet, "ints", [(0, 1), (1, 0)])
    order.append("packet")
    send("over_behind", "over", 1, 1)
    send("over_ahead", "over", 1, -1)
    send("own_over", "own_behind", 1, 1)
    send("ahead_over", "ahead_ahead", 1, -1)
    send("behind_over", "behind_behind", 1, 1)
    send("over_over", "over_behind", 1, 1)
    along = {"own": 0, "ahead": 1, "over": 2, "behind": 3}
    pieces = [(0, at, held[name]) for name, at in along.items()]
    for name, at in along.items():
        pieces += [(1, at, held[name + "_ahead"]), (3, at, held[name + "_behind"]), (2, at, held[name + "_over"])]
    return pieces, held["packet"]


def assemble(copies, base_ref, *refs):
    arrays, table, sems = refs[:-2], refs[-2], refs[-1]
    dmas = []
    for n, slot in enumerate(copies):
        rows = arrays[n].shape[0]
        dmas.append(pltpu.make_async_copy(arrays[n], table.at[pl.ds(base_ref[slot], rows)], sems.at[n]))
    for dma in dmas:
        dma.start()
    for dma in dmas:
        dma.wait()


def kernel(
    steps, pairs, slots,
    table, src_ref, tgt_ref, sign_ref, vb_ref, off_ref, bs_ref, keep_hbm, give_hbm,
    g_ref, y_ref, vhi_ref, vlo_ref, acc_ref, sem_out,
):
    v = vb_ref[...]
    high = v.astype(jnp.bfloat16)
    vhi_ref[...] = high
    vlo_ref[...] = (v - high.astype(jnp.float32)).astype(jnp.bfloat16)
    acc_ref[...] = jnp.zeros_like(acc_ref)
    rows = GROUP * pairs

    def fetch(step, buffer):
        for r in range(rows):
            g_ref[buffer, r] = table[src_ref[step * rows + r]]

    def mix(step, buffer):
        flat = g_ref.at[buffer].reshape(rows * slots, LANES)
        sign = sign_ref[pl.ds(step, 1), :].astype(jnp.bfloat16)
        left_hi = vhi_ref[...] * sign
        left_lo = vlo_ref[...] * sign
        g = jnp.concatenate([flat[pl.ds(q, rows, stride=slots), :] for q in range(slots)], 1)
        hi = g.astype(jnp.bfloat16)
        lo = (g - hi.astype(jnp.float32)).astype(jnp.bfloat16)
        got = jnp.dot(
            jnp.concatenate([left_hi, left_lo, left_hi], 1),
            jnp.concatenate([hi, hi, lo], 0),
            preferred_element_type=jnp.float32,
        )
        for q in range(slots):
            part = got[:, q * LANES : (q + 1) * LANES]
            y_ref[:, q, pl.ds(step * GROUP, GROUP), :] = part.reshape(pairs, GROUP, LANES)

    fetch(0, 0)

    def two(half, carry):
        step = half * 2
        fetch(step + 1, 1)
        mix(step, 0)
        fetch(jnp.minimum(step + 2, steps - 1), 0)
        mix(step + 1, 1)
        return carry

    lax.fori_loop(0, steps // 2, two, 0)
    lines = lax.broadcasted_iota(jnp.int32, (LANES, LANES), 0)
    tiles = acc_ref.shape[0]

    def place(pair):
        found = []
        for q in range(slots):
            t = tgt_ref[pair * slots + q]
            spot = tgt_ref[(pairs + pair) * slots + q]
            off = off_ref[pl.ds(pair * tiles + t, 1), :]
            sgn = bs_ref[pl.ds(pair * tiles + t, 1), :].astype(jnp.float32)
            hot = jnp.where(lines == off, sgn, 0.0).astype(jnp.bfloat16)
            y = y_ref[pair, q]
            hi = y.astype(jnp.bfloat16)
            lo = (y - hi.astype(jnp.float32)).astype(jnp.bfloat16)
            left = jnp.concatenate([hi, lo], 1)
            right = jnp.concatenate([hot, hot], 0)
            found.append((spot, jnp.dot(left, right, preferred_element_type=jnp.float32)))
        for spot, value in found:
            acc_ref[spot] += value

    def some_pairs(part, carry):
        for n in range(UNROLL):
            place(part * UNROLL + n)
        return carry

    lax.fori_loop(0, pairs // UNROLL, some_pairs, 0)
    half = tiles // 2
    store_give = pltpu.make_async_copy(acc_ref.at[pl.ds(half, half)], give_hbm, sem_out.at[0])
    store_keep = pltpu.make_async_copy(acc_ref.at[pl.ds(0, half)], keep_hbm, sem_out.at[1])
    store_give.start()
    store_keep.start()
    store_give.wait()
    store_keep.wait()


def local(ci_vector, integrals, alpha_source, alpha_sign, beta_tiles, beta_offsets, beta_sign):
    rows_b, cols_a = ci_vector.shape
    pairs, tiles, tile = beta_offsets.shape
    slots = rows_b // tile
    ints = lax.axis_size("ints")
    mine = lax.axis_index("ints")
    cols = cols_a // ints
    alpha = lax.axis_index("alpha")
    x, z = alpha // RING, alpha % RING

    beta = lax.axis_index("beta")
    betas = lax.axis_size("beta")
    rings = betas // CORES
    y, core = beta // CORES, beta % CORES

    columns = ci_vector.T.reshape(cols_a, slots, tile)

    swap = [(0, 1), (1, 0)]
    first = mine == 0
    share = integrals.shape[0]
    both = jnp.stack([alpha_source, alpha_sign]).astype(jnp.float32)
    keep = lax.dynamic_slice_in_dim(both, mine * cols, cols, 2)
    give = lax.dynamic_slice_in_dim(both, (1 - mine) * cols, cols, 2)
    packet = jnp.concatenate([give.reshape(2 * share, cols), jnp.pad(integrals, ((0, 0), (0, cols - pairs)))], 0)
    pieces, packet = spread(columns, packet)
    got = packet[: 2 * share].reshape(2, share, cols)
    v_got = packet[2 * share :, :pairs]
    full = jnp.concatenate([jnp.where(first, keep, got), jnp.where(first, got, keep)], 1)
    v = jnp.concatenate([jnp.where(first, integrals, v_got), jnp.where(first, v_got, integrals)], 0)
    flat = full.transpose(0, 2, 1).reshape(2, cols * pairs)
    source = flat[0].astype(jnp.int32)
    steps = cols // GROUP
    sign = flat[1].reshape(steps, GROUP * pairs)
    eye = jnp.eye(GROUP, dtype=jnp.float32)
    vb = (v.T[:, None, None, :] * eye[None, :, :, None]).reshape(pairs * GROUP, GROUP * pairs)

    wanted = beta * slots + jnp.arange(slots, dtype=jnp.int32)
    hit = beta_tiles[:, :, None] == wanted[None, None, :]
    target = jnp.sum(jnp.where(hit, jnp.arange(tiles, dtype=jnp.int32)[None, :, None], 0), axis=1).reshape(-1)
    owner = target // slots
    away = (owner // CORES - y) % rings
    spot = ((owner % CORES) ^ core) * (tiles // CORES) + away * slots + target % slots
    target = jnp.concatenate([target, spot])

    arrays = [array for _, _, array in pieces]
    copies = [on_one * RING + on_zero for on_one, on_zero, _ in pieces]
    d = jnp.arange(RING * RING, dtype=jnp.int32)
    dx = jnp.where(core == 0, d // RING, d % RING)
    dz = jnp.where(core == 0, d % RING, d // RING)
    base = (((x + dx) % RING) * RING + (z + dz) % RING) * cols_a

    smem = pl.BlockSpec(memory_space=pltpu.SMEM)
    vmem = pl.BlockSpec(memory_space=pltpu.VMEM)
    hbm = pl.BlockSpec(memory_space=pl.ANY)
    table = pl.pallas_call(
        functools.partial(assemble, tuple(copies)),
        out_shape=jax.ShapeDtypeStruct((lax.axis_size("alpha") * cols_a, slots, tile), jnp.float32),
        in_specs=[smem] + [hbm] * len(arrays),
        out_specs=vmem,
        scratch_shapes=[pltpu.SemaphoreType.DMA((len(copies),))],
        compiler_params=pltpu.CompilerParams(vmem_limit_bytes=12 * 1024 * 1024),
        name="assemble",
    )(base, *arrays)
    width = cols // CHUNKS
    offsets = beta_offsets.reshape(pairs * tiles, tile)
    signs = beta_sign.reshape(pairs * tiles, tile)
    across = [(b, b ^ 1) for b in range(betas)]
    half = jax.ShapeDtypeStruct((tiles // CORES, width, tile), jnp.float32)
    part_steps = steps // CHUNKS
    sums = []
    for chunk in range(CHUNKS):
        keep, give = pl.pallas_call(
            functools.partial(kernel, part_steps, pairs, slots),
            out_shape=(half, half),
            in_specs=[vmem] + [smem] * 2 + [vmem] * 4,
            out_specs=(hbm, hbm),
            scratch_shapes=[
                pltpu.VMEM((2, GROUP * pairs, slots, tile), jnp.float32),
                pltpu.VMEM((pairs, slots, width, tile), jnp.float32),
                pltpu.VMEM((GROUP * pairs, GROUP * pairs), jnp.bfloat16),
                pltpu.VMEM((GROUP * pairs, GROUP * pairs), jnp.bfloat16),
                pltpu.VMEM((tiles, width, tile), jnp.float32),
                pltpu.SemaphoreType.DMA((2,)),
            ],
            compiler_params=pltpu.CompilerParams(vmem_limit_bytes=12 * 1024 * 1024),
            cost_estimate=pl.CostEstimate(flops=4 * 10**9, bytes_accessed=2**23, transcendentals=0),
            name="sigma_partial",
        )(
            table,
            lax.slice_in_dim(source, chunk * width * pairs, (chunk + 1) * width * pairs),
            target,
            lax.slice_in_dim(sign, chunk * part_steps, (chunk + 1) * part_steps),
            vb,
            offsets,
            signs,
        )
        came = lax.ppermute(give, "beta", across)
        total = keep[:slots] + came[:slots]
        for far in (2, 1, 3):
            pairs_y = [(b, (b + far * CORES) % betas) for b in range(betas)]
            part = keep[far * slots : (far + 1) * slots] + came[far * slots : (far + 1) * slots]
            total = total + lax.ppermute(part, "beta", pairs_y)
        sums.append((total, lax.ppermute(total, "ints", swap)))
    mine_all = jnp.concatenate([m for m, _ in sums], 1)
    other_all = jnp.concatenate([o for _, o in sums], 1)
    joined = jnp.concatenate([jnp.where(first, mine_all, other_all), jnp.where(first, other_all, mine_all)], 1)
    return joined.transpose(0, 2, 1).reshape(rows_b, cols_a)


def solution(mesh):
    return jax.shard_map(
        local,
        mesh=mesh,
        in_specs=(
            P("beta", "alpha"),
            P("ints", None),
            P("ints", "alpha"),
            P("ints", "alpha"),
            P(),
            P(),
            P(),
        ),
        out_specs=P("beta", "alpha"),
        check_vma=False,
    )
```

```python
import functools

import jax
import jax.numpy as jnp
from jax import lax
from jax.experimental import pallas as pl
from jax.experimental.pallas import tpu as pltpu
from jax.sharding import PartitionSpec as P

LANES = 128
GROUP = 8
RING = 4
CORES = 2
CHUNKS = 2
UNROLL = 4
FLIGHT = 5
AXES = ("alpha", "beta", "ints")


def device(x, z, y, core):
    ints = lax.axis_size("ints")
    x, z = x % RING, z % (RING * ints)
    alpha = x * RING + z % RING
    return (alpha * lax.axis_size("beta") + y * CORES + core) * ints + z // RING


def move(value, axis, step):
    pairs = []
    for x in range(lax.axis_size("alpha") // RING):
        for z in range(RING * lax.axis_size("ints")):
            for y in range(lax.axis_size("beta") // CORES):
                for core in range(CORES):
                    dx, dz = (step, 0) if axis != core else (0, step)
                    pairs.append((device(x, z, y, core), device(x + dx, z + dz, y, core)))
    return lax.ppermute(value, AXES, pairs)


PLAN = (
    ("own_behind", "own", 1, 1, ()),
    ("ahead", "own", 0, -1, ()),
    ("behind", "own", 0, 1, ()),
    ("packet", "packet", 0, 1, ()),
    ("over", "ahead", 0, -1, ("ahead",)),
    ("ahead_behind", "ahead", 1, 1, ()),
    ("ahead_ahead", "ahead", 1, -1, ("own_behind",)),
    ("behind_behind", "behind", 1, 1, ("behind",)),
    ("behind_ahead", "behind", 1, -1, ("packet",)),
    ("own_over", "own_behind", 1, 1, ("over",)),
    ("over_behind", "over", 1, 1, ("ahead_behind",)),
    ("over_ahead", "over", 1, -1, ("ahead_ahead",)),
    ("ahead_over", "ahead_behind", 1, 1, ("behind_behind",)),
    ("over_over", "over_ahead", 1, -1, ("over_ahead",)),
    ("own_ahead", "own", 1, -1, ("behind_ahead",)),
    ("behind_over", "behind_behind", 1, 1, ("own_over",)),
)
LAST = ("ahead_over", "over_over", "own_ahead", "behind_over",)
ALONG = {"own": 0, "ahead": 1, "over": 2, "behind": 3}
ACROSS = {"": 0, "_ahead": 1, "_over": 2, "_behind": 3}


def spread(block, packet):
    held = {"own": block}
    for name, source, axis, step, waits in PLAN:
        value = packet if name == "packet" else held[source]
        if waits:
            value = lax.optimization_barrier((value, *[held[w] for w in waits]))[0]
        if name == "packet":
            held[name] = lax.ppermute(value, "ints", [(0, 1), (1, 0)])
        else:
            held[name] = move(value, axis, step)
    packet = held.pop("packet")
    return held, packet


def slot_of(name):
    first, _, second = name.partition("_")
    return ACROSS["_" + second if second else ""] * RING + ALONG[first]


def assemble(copies, held, base_ref, *refs):
    arrays, table, sems = refs[: len(copies)], refs[-2], refs[-1]
    dmas = []
    for n, slot in enumerate(copies):
        rows = arrays[n].shape[0]
        dmas.append(pltpu.make_async_copy(arrays[n], table.at[pl.ds(base_ref[slot], rows)], sems.at[n]))
    for dma in dmas:
        dma.start()
    for dma in dmas:
        dma.wait()


def kernel(
    steps, pairs, slots,
    table, src_ref, tgt_ref, sign_ref, vb_ref, off_ref, bs_ref, keep_hbm, give_hbm,
    g_ref, y_ref, vhi_ref, vlo_ref, acc_ref, sem_out,
):
    v = vb_ref[...]
    high = v.astype(jnp.bfloat16)
    vhi_ref[...] = high
    vlo_ref[...] = (v - high.astype(jnp.float32)).astype(jnp.bfloat16)
    acc_ref[...] = jnp.zeros_like(acc_ref)
    rows = GROUP * pairs

    def fetch(step, buffer):
        for r in range(rows):
            g_ref[buffer, r] = table[src_ref[step * rows + r]]

    def mix(step, buffer):
        flat = g_ref.at[buffer].reshape(rows * slots, LANES)
        sign = sign_ref[pl.ds(step, 1), :].astype(jnp.bfloat16)
        left_hi = vhi_ref[...] * sign
        left_lo = vlo_ref[...] * sign
        g = jnp.concatenate([flat[pl.ds(q, rows, stride=slots), :] for q in range(slots)], 1)
        hi = g.astype(jnp.bfloat16)
        lo = (g - hi.astype(jnp.float32)).astype(jnp.bfloat16)
        got = jnp.dot(
            jnp.concatenate([left_hi, left_lo, left_hi], 1),
            jnp.concatenate([hi, hi, lo], 0),
            preferred_element_type=jnp.float32,
        )
        for q in range(slots):
            part = got[:, q * LANES : (q + 1) * LANES]
            y_ref[:, q, pl.ds(step * GROUP, GROUP), :] = part.reshape(pairs, GROUP, LANES)

    fetch(0, 0)

    def two(half, carry):
        step = half * 2
        fetch(step + 1, 1)
        mix(step, 0)
        fetch(jnp.minimum(step + 2, steps - 1), 0)
        mix(step + 1, 1)
        return carry

    lax.fori_loop(0, steps // 2, two, 0)
    lines = lax.broadcasted_iota(jnp.int32, (LANES, LANES), 0)
    tiles = acc_ref.shape[0]

    def place(pair):
        found = []
        for q in range(slots):
            t = tgt_ref[pair * slots + q]
            spot = tgt_ref[(pairs + pair) * slots + q]
            off = off_ref[pl.ds(pair * tiles + t, 1), :]
            sgn = bs_ref[pl.ds(pair * tiles + t, 1), :].astype(jnp.float32)
            hot = jnp.where(lines == off, sgn, 0.0).astype(jnp.bfloat16)
            y = y_ref[pair, q]
            hi = y.astype(jnp.bfloat16)
            lo = (y - hi.astype(jnp.float32)).astype(jnp.bfloat16)
            left = jnp.concatenate([hi, lo], 1)
            right = jnp.concatenate([hot, hot], 0)
            found.append((spot, jnp.dot(left, right, preferred_element_type=jnp.float32)))
        for spot, value in found:
            acc_ref[spot] += value

    def some_pairs(part, carry):
        for n in range(UNROLL):
            place(part * UNROLL + n)
        return carry

    lax.fori_loop(0, pairs // UNROLL, some_pairs, 0)
    half = tiles // 2
    store_give = pltpu.make_async_copy(acc_ref.at[pl.ds(half, half)], give_hbm, sem_out.at[0])
    store_keep = pltpu.make_async_copy(acc_ref.at[pl.ds(0, half)], keep_hbm, sem_out.at[1])
    store_give.start()
    store_keep.start()
    store_give.wait()
    store_keep.wait()


def local(ci_vector, integrals, alpha_source, alpha_sign, beta_tiles, beta_offsets, beta_sign):
    rows_b, cols_a = ci_vector.shape
    pairs, tiles, tile = beta_offsets.shape
    slots = rows_b // tile
    ints = lax.axis_size("ints")
    mine = lax.axis_index("ints")
    cols = cols_a // ints
    alpha = lax.axis_index("alpha")
    x, z = alpha // RING, alpha % RING

    beta = lax.axis_index("beta")
    betas = lax.axis_size("beta")
    rings = betas // CORES
    y, core = beta // CORES, beta % CORES

    columns = ci_vector.T.reshape(cols_a, slots, tile)

    swap = [(0, 1), (1, 0)]
    first = mine == 0
    share = integrals.shape[0]
    both = jnp.stack([alpha_source, alpha_sign]).astype(jnp.float32)
    keep = lax.dynamic_slice_in_dim(both, mine * cols, cols, 2)
    give = lax.dynamic_slice_in_dim(both, (1 - mine) * cols, cols, 2)
    packet = jnp.concatenate([give.reshape(2 * share, cols), jnp.pad(integrals, ((0, 0), (0, cols - pairs)))], 0)
    pieces, packet = spread(columns, packet)
    got = packet[: 2 * share].reshape(2, share, cols)
    v_got = packet[2 * share :, :pairs]
    full = jnp.concatenate([jnp.where(first, keep, got), jnp.where(first, got, keep)], 1)
    v = jnp.concatenate([jnp.where(first, integrals, v_got), jnp.where(first, v_got, integrals)], 0)
    flat = full.transpose(0, 2, 1).reshape(2, cols * pairs)
    source = flat[0].astype(jnp.int32)
    steps = cols // GROUP
    sign = flat[1].reshape(steps, GROUP * pairs)
    eye = jnp.eye(GROUP, dtype=jnp.float32)
    vb = (v.T[:, None, None, :] * eye[None, :, :, None]).reshape(pairs * GROUP, GROUP * pairs)

    wanted = beta * slots + jnp.arange(slots, dtype=jnp.int32)
    hit = beta_tiles[:, :, None] == wanted[None, None, :]
    target = jnp.sum(jnp.where(hit, jnp.arange(tiles, dtype=jnp.int32)[None, :, None], 0), axis=1).reshape(-1)
    owner = target // slots
    away = (owner // CORES - y) % rings
    spot = ((owner % CORES) ^ core) * (tiles // CORES) + away * slots + target % slots
    target = jnp.concatenate([target, spot])

    d = jnp.arange(RING * RING, dtype=jnp.int32)
    dx = jnp.where(core == 0, d // RING, d % RING)
    dz = jnp.where(core == 0, d % RING, d // RING)
    base = (((x + dx) % RING) * RING + (z + dz) % RING) * cols_a

    smem = pl.BlockSpec(memory_space=pltpu.SMEM)
    vmem = pl.BlockSpec(memory_space=pltpu.VMEM)
    hbm = pl.BlockSpec(memory_space=pl.ANY)
    table = None
    for names in (tuple(n for n in pieces if n not in LAST), LAST):
        old = [] if table is None else [table]
        table = pl.pallas_call(
            functools.partial(assemble, tuple(slot_of(n) for n in names), len(old)),
            out_shape=jax.ShapeDtypeStruct((lax.axis_size("alpha") * cols_a, slots, tile), jnp.float32),
            in_specs=[smem] + [hbm] * len(names) + [vmem] * len(old),
            out_specs=vmem,
            scratch_shapes=[pltpu.SemaphoreType.DMA((len(names),))],
            input_output_aliases={1 + len(names): 0} if old else {},
            compiler_params=pltpu.CompilerParams(vmem_limit_bytes=12 * 1024 * 1024),
            name="assemble",
        )(base, *[pieces[n] for n in names], *old)
    width = cols // CHUNKS
    offsets = beta_offsets.reshape(pairs * tiles, tile)
    signs = beta_sign.reshape(pairs * tiles, tile)
    across = [(b, b ^ 1) for b in range(betas)]
    half = jax.ShapeDtypeStruct((tiles // CORES, width, tile), jnp.float32)
    part_steps = steps // CHUNKS
    sums = []
    for chunk in range(CHUNKS):
        keep, give = pl.pallas_call(
            functools.partial(kernel, part_steps, pairs, slots),
            out_shape=(half, half),
            in_specs=[vmem] + [smem] * 2 + [vmem] * 4,
            out_specs=(hbm, hbm),
            scratch_shapes=[
                pltpu.VMEM((2, GROUP * pairs, slots, tile), jnp.float32),
                pltpu.VMEM((pairs, slots, width, tile), jnp.float32),
                pltpu.VMEM((GROUP * pairs, GROUP * pairs), jnp.bfloat16),
                pltpu.VMEM((GROUP * pairs, GROUP * pairs), jnp.bfloat16),
                pltpu.VMEM((tiles, width, tile), jnp.float32),
                pltpu.SemaphoreType.DMA((2,)),
            ],
            compiler_params=pltpu.CompilerParams(vmem_limit_bytes=12 * 1024 * 1024),
            cost_estimate=pl.CostEstimate(flops=4 * 10**9, bytes_accessed=2**23, transcendentals=0),
            name="sigma_partial",
        )(
            table,
            lax.slice_in_dim(source, chunk * width * pairs, (chunk + 1) * width * pairs),
            target,
            lax.slice_in_dim(sign, chunk * part_steps, (chunk + 1) * part_steps),
            vb,
            offsets,
            signs,
        )
        came = lax.ppermute(give, "beta", across)
        total = keep[:slots] + came[:slots]
        for far in (2, 1, 3):
            pairs_y = [(b, (b + far * CORES) % betas) for b in range(betas)]
            part = keep[far * slots : (far + 1) * slots] + came[far * slots : (far + 1) * slots]
            total = total + lax.ppermute(part, "beta", pairs_y)
        sums.append((total, lax.ppermute(total, "ints", swap)))
    mine_all = jnp.concatenate([m for m, _ in sums], 1)
    other_all = jnp.concatenate([o for _, o in sums], 1)
    joined = jnp.concatenate([jnp.where(first, mine_all, other_all), jnp.where(first, other_all, mine_all)], 1)
    return joined.transpose(0, 2, 1).reshape(rows_b, cols_a)


def solution(mesh):
    return jax.shard_map(
        local,
        mesh=mesh,
        in_specs=(
            P("beta", "alpha"),
            P("ints", None),
            P("ints", "alpha"),
            P("ints", "alpha"),
            P(),
            P(),
            P(),
        ),
        out_specs=P("beta", "alpha"),
        check_vma=False,
    )
```

```python
import functools

import jax
import jax.numpy as jnp
from jax import lax
from jax.experimental import pallas as pl
from jax.experimental.pallas import tpu as pltpu
from jax.sharding import PartitionSpec as P

LANES = 128
GROUP = 8
RING = 4
CORES = 2
CHUNKS = 2
UNROLL = 8
MIXES = 4
FLIGHT = 5
AXES = ("alpha", "beta", "ints")


def device(x, z, y, core):
    ints = lax.axis_size("ints")
    x, z = x % RING, z % (RING * ints)
    alpha = x * RING + z % RING
    return (alpha * lax.axis_size("beta") + y * CORES + core) * ints + z // RING


def move(value, axis, step):
    pairs = []
    for x in range(lax.axis_size("alpha") // RING):
        for z in range(RING * lax.axis_size("ints")):
            for y in range(lax.axis_size("beta") // CORES):
                for core in range(CORES):
                    dx, dz = (step, 0) if axis != core else (0, step)
                    pairs.append((device(x, z, y, core), device(x + dx, z + dz, y, core)))
    return lax.ppermute(value, AXES, pairs)


PLAN = (
    ("own_behind", "own", 1, 1, ()),
    ("ahead", "own", 0, -1, ()),
    ("behind", "own", 0, 1, ()),
    ("packet", "packet", 0, 1, ()),
    ("over", "ahead", 0, -1, ("ahead",)),
    ("ahead_behind", "ahead", 1, 1, ()),
    ("ahead_ahead", "ahead", 1, -1, ("own_behind",)),
    ("behind_behind", "behind", 1, 1, ("behind",)),
    ("behind_ahead", "behind", 1, -1, ("packet",)),
    ("own_over", "own_behind", 1, 1, ("over",)),
    ("over_behind", "over", 1, 1, ("ahead_behind",)),
    ("over_ahead", "over", 1, -1, ("ahead_ahead",)),
    ("ahead_over", "ahead_behind", 1, 1, ("behind_behind",)),
    ("over_over", "over_ahead", 1, -1, ("over_ahead",)),
    ("own_ahead", "own", 1, -1, ("behind_ahead",)),
    ("behind_over", "behind_behind", 1, 1, ("own_over",)),
)
LAST = ("ahead_over", "over_over", "own_ahead", "behind_over",)
ALONG = {"own": 0, "ahead": 1, "over": 2, "behind": 3}
ACROSS = {"": 0, "_ahead": 1, "_over": 2, "_behind": 3}


def spread(block, packet):
    held = {"own": block}
    for name, source, axis, step, waits in PLAN:
        value = packet if name == "packet" else held[source]
        if waits:
            value = lax.optimization_barrier((value, *[held[w] for w in waits]))[0]
        if name == "packet":
            held[name] = lax.ppermute(value, "ints", [(0, 1), (1, 0)])
        else:
            held[name] = move(value, axis, step)
    packet = held.pop("packet")
    return held, packet


def slot_of(name):
    first, _, second = name.partition("_")
    return ACROSS["_" + second if second else ""] * RING + ALONG[first]


def assemble(copies, base_ref, *refs):
    arrays, table, sems = refs[: len(copies)], refs[-2], refs[-1]
    dmas = []
    for n, slot in enumerate(copies):
        rows = arrays[n].shape[0]
        dmas.append(pltpu.make_async_copy(arrays[n], table.at[pl.ds(base_ref[slot], rows)], sems.at[n]))
    for dma in dmas:
        dma.start()
    for dma in dmas:
        dma.wait()


def kernel(steps, pairs, slots, copies, *refs):
    src_ref, tgt_ref, sign_ref, vb_ref, off_ref, bs_ref, table = refs[:7]
    late = len(copies)
    keep_hbm, give_hbm, g_ref, y_ref, vhi_ref, vlo_ref, acc_ref, sem_out = refs[-8 - bool(late) :][:8]
    dmas = []
    if late:
        base_ref, arrays, table, sems = refs[7], refs[8 : 8 + late], refs[8 + late], refs[-1]
        for n, slot in enumerate(copies):
            rows = arrays[n].shape[0]
            dmas.append(pltpu.make_async_copy(arrays[n], table.at[pl.ds(base_ref[slot], rows)], sems.at[n]))
    for dma in dmas:
        dma.start()
    v = vb_ref[...]
    high = v.astype(jnp.bfloat16)
    vhi_ref[...] = high
    vlo_ref[...] = (v - high.astype(jnp.float32)).astype(jnp.bfloat16)
    acc_ref[...] = jnp.zeros_like(acc_ref)
    for dma in dmas:
        dma.wait()
    rows = GROUP * pairs

    def fetch(step, buffer):
        for r in range(rows):
            g_ref[buffer, r] = table[src_ref[step * rows + r]]

    def mix(step, buffer):
        flat = g_ref.at[buffer].reshape(rows * slots, LANES)
        sign = sign_ref[pl.ds(step, 1), :].astype(jnp.bfloat16)
        left_hi = vhi_ref[...] * sign
        left_lo = vlo_ref[...] * sign
        g = jnp.concatenate([flat[pl.ds(q, rows, stride=slots), :] for q in range(slots)], 1)
        hi = g.astype(jnp.bfloat16)
        lo = (g - hi.astype(jnp.float32)).astype(jnp.bfloat16)
        got = jnp.dot(
            jnp.concatenate([left_hi, left_lo, left_hi], 1),
            jnp.concatenate([hi, hi, lo], 0),
            preferred_element_type=jnp.float32,
        )
        for q in range(slots):
            part = got[:, q * LANES : (q + 1) * LANES]
            y_ref[:, q, pl.ds(step * GROUP, GROUP), :] = part.reshape(pairs, GROUP, LANES)

    fetch(0, 0)

    def some_steps(part, carry):
        for n in range(MIXES):
            step = part * MIXES + n
            fetch(jnp.minimum(step + 1, steps - 1), (n + 1) % 2)
            mix(step, n % 2)
        return carry

    lax.fori_loop(0, steps // MIXES, some_steps, 0)
    lines = lax.broadcasted_iota(jnp.int32, (LANES, LANES), 0)
    tiles = acc_ref.shape[0]

    def place(pair):
        found = []
        for q in range(slots):
            t = tgt_ref[pair * slots + q]
            spot = tgt_ref[(pairs + pair) * slots + q]
            off = off_ref[pl.ds(pair * tiles + t, 1), :]
            sgn = bs_ref[pl.ds(pair * tiles + t, 1), :].astype(jnp.float32)
            hot = jnp.where(lines == off, sgn, 0.0).astype(jnp.bfloat16)
            y = y_ref[pair, q]
            hi = y.astype(jnp.bfloat16)
            lo = (y - hi.astype(jnp.float32)).astype(jnp.bfloat16)
            left = jnp.concatenate([hi, lo], 1)
            right = jnp.concatenate([hot, hot], 0)
            found.append((spot, jnp.dot(left, right, preferred_element_type=jnp.float32)))
        for spot, value in found:
            acc_ref[spot] += value

    def some_pairs(part, carry):
        for n in range(UNROLL):
            place(part * UNROLL + n)
        return carry

    lax.fori_loop(0, pairs // UNROLL, some_pairs, 0)
    half = tiles // 2
    store_give = pltpu.make_async_copy(acc_ref.at[pl.ds(half, half)], give_hbm, sem_out.at[0])
    store_keep = pltpu.make_async_copy(acc_ref.at[pl.ds(0, half)], keep_hbm, sem_out.at[1])
    store_give.start()
    store_keep.start()
    store_give.wait()
    store_keep.wait()


def local(ci_vector, integrals, alpha_source, alpha_sign, beta_tiles, beta_offsets, beta_sign):
    rows_b, cols_a = ci_vector.shape
    pairs, tiles, tile = beta_offsets.shape
    slots = rows_b // tile
    ints = lax.axis_size("ints")
    mine = lax.axis_index("ints")
    cols = cols_a // ints
    alpha = lax.axis_index("alpha")
    x, z = alpha // RING, alpha % RING

    beta = lax.axis_index("beta")
    betas = lax.axis_size("beta")
    rings = betas // CORES
    y, core = beta // CORES, beta % CORES

    columns = ci_vector.T.reshape(cols_a, slots, tile)

    swap = [(0, 1), (1, 0)]
    first = mine == 0
    share = integrals.shape[0]
    both = jnp.stack([alpha_source, alpha_sign]).astype(jnp.float32)
    keep = lax.dynamic_slice_in_dim(both, mine * cols, cols, 2)
    give = lax.dynamic_slice_in_dim(both, (1 - mine) * cols, cols, 2)
    packet = jnp.concatenate([give.reshape(2 * share, cols), jnp.pad(integrals, ((0, 0), (0, cols - pairs)))], 0)
    pieces, packet = spread(columns, packet)
    got = packet[: 2 * share].reshape(2, share, cols)
    v_got = packet[2 * share :, :pairs]
    full = jnp.concatenate([jnp.where(first, keep, got), jnp.where(first, got, keep)], 1)
    v = jnp.concatenate([jnp.where(first, integrals, v_got), jnp.where(first, v_got, integrals)], 0)
    flat = full.transpose(0, 2, 1).reshape(2, cols * pairs)
    source = flat[0].astype(jnp.int32)
    steps = cols // GROUP
    sign = flat[1].reshape(steps, GROUP * pairs)
    eye = jnp.eye(GROUP, dtype=jnp.float32)
    vb = (v.T[:, None, None, :] * eye[None, :, :, None]).reshape(pairs * GROUP, GROUP * pairs)

    wanted = beta * slots + jnp.arange(slots, dtype=jnp.int32)
    hit = beta_tiles[:, :, None] == wanted[None, None, :]
    target = jnp.sum(jnp.where(hit, jnp.arange(tiles, dtype=jnp.int32)[None, :, None], 0), axis=1).reshape(-1)
    owner = target // slots
    away = (owner // CORES - y) % rings
    spot = ((owner % CORES) ^ core) * (tiles // CORES) + away * slots + target % slots
    target = jnp.concatenate([target, spot])

    d = jnp.arange(RING * RING, dtype=jnp.int32)
    dx = jnp.where(core == 0, d // RING, d % RING)
    dz = jnp.where(core == 0, d % RING, d // RING)
    base = (((x + dx) % RING) * RING + (z + dz) % RING) * cols_a

    smem = pl.BlockSpec(memory_space=pltpu.SMEM)
    vmem = pl.BlockSpec(memory_space=pltpu.VMEM)
    hbm = pl.BlockSpec(memory_space=pl.ANY)
    whole = jax.ShapeDtypeStruct((lax.axis_size("alpha") * cols_a, slots, tile), jnp.float32)
    early = tuple(n for n in pieces if n not in LAST)
    table = pl.pallas_call(
        functools.partial(assemble, tuple(slot_of(n) for n in early)),
        out_shape=whole,
        in_specs=[smem] + [hbm] * len(early),
        out_specs=vmem,
        scratch_shapes=[pltpu.SemaphoreType.DMA((len(early),))],
        compiler_params=pltpu.CompilerParams(vmem_limit_bytes=12 * 1024 * 1024),
        name="assemble",
    )(base, *[pieces[n] for n in early])
    width = cols // CHUNKS
    offsets = beta_offsets.reshape(pairs * tiles, tile)
    signs = beta_sign.reshape(pairs * tiles, tile)
    across = [(b, b ^ 1) for b in range(betas)]
    half = jax.ShapeDtypeStruct((tiles // CORES, width, tile), jnp.float32)
    part_steps = steps // CHUNKS
    sums = []
    for chunk in range(CHUNKS):
        late = LAST if chunk == 0 else ()
        outs = pl.pallas_call(
            functools.partial(kernel, part_steps, pairs, slots, tuple(slot_of(n) for n in late)),
            out_shape=((whole,) if late else ()) + (half, half),
            in_specs=[smem] * 2 + [vmem] * 5 + [smem] * bool(late) + [hbm] * len(late),
            out_specs=((vmem,) if late else ()) + (hbm, hbm),
            scratch_shapes=[
                pltpu.VMEM((2, GROUP * pairs, slots, tile), jnp.float32),
                pltpu.VMEM((pairs, slots, width, tile), jnp.float32),
                pltpu.VMEM((GROUP * pairs, GROUP * pairs), jnp.bfloat16),
                pltpu.VMEM((GROUP * pairs, GROUP * pairs), jnp.bfloat16),
                pltpu.VMEM((tiles, width, tile), jnp.float32),
                pltpu.SemaphoreType.DMA((2,)),
            ]
            + [pltpu.SemaphoreType.DMA((len(late),))] * bool(late),
            input_output_aliases={6: 0} if late else {},
            compiler_params=pltpu.CompilerParams(vmem_limit_bytes=12 * 1024 * 1024),
            cost_estimate=pl.CostEstimate(flops=4 * 10**9, bytes_accessed=2**23, transcendentals=0),
            name="sigma_partial",
        )(
            lax.slice_in_dim(source, chunk * width * pairs, (chunk + 1) * width * pairs),
            target,
            lax.slice_in_dim(sign, chunk * part_steps, (chunk + 1) * part_steps),
            vb,
            offsets,
            signs,
            table,
            *([base] * bool(late)),
            *[pieces[n] for n in late],
        )
        if late:
            table, keep, give = outs
        else:
            keep, give = outs
        came = lax.ppermute(give, "beta", across)
        total = keep[:slots] + came[:slots]
        for far in (2, 1, 3):
            pairs_y = [(b, (b + far * CORES) % betas) for b in range(betas)]
            part = keep[far * slots : (far + 1) * slots] + came[far * slots : (far + 1) * slots]
            total = total + lax.ppermute(part, "beta", pairs_y)
        sums.append((total, lax.ppermute(total, "ints", swap)))
    mine_all = jnp.concatenate([m for m, _ in sums], 1)
    other_all = jnp.concatenate([o for _, o in sums], 1)
    joined = jnp.concatenate([jnp.where(first, mine_all, other_all), jnp.where(first, other_all, mine_all)], 1)
    return joined.transpose(0, 2, 1).reshape(rows_b, cols_a)


def solution(mesh):
    return jax.shard_map(
        local,
        mesh=mesh,
        in_specs=(
            P("beta", "alpha"),
            P("ints", None),
            P("ints", "alpha"),
            P("ints", "alpha"),
            P(),
            P(),
            P(),
        ),
        out_specs=P("beta", "alpha"),
        check_vma=False,
    )
```

```python
import functools

import jax
import jax.numpy as jnp
from jax import lax
from jax.experimental import pallas as pl
from jax.experimental.pallas import tpu as pltpu
from jax.sharding import PartitionSpec as P

LANES = 128
GROUP = 8
RING = 4
CORES = 2
CHUNKS = 2
UNROLL = 16
MIXES = 8
FLIGHT = 5
AXES = ("alpha", "beta", "ints")


def device(x, z, y, core):
    ints = lax.axis_size("ints")
    x, z = x % RING, z % (RING * ints)
    alpha = x * RING + z % RING
    return (alpha * lax.axis_size("beta") + y * CORES + core) * ints + z // RING


def move(value, axis, step):
    pairs = []
    for x in range(lax.axis_size("alpha") // RING):
        for z in range(RING * lax.axis_size("ints")):
            for y in range(lax.axis_size("beta") // CORES):
                for core in range(CORES):
                    dx, dz = (step, 0) if axis != core else (0, step)
                    pairs.append((device(x, z, y, core), device(x + dx, z + dz, y, core)))
    return lax.ppermute(value, AXES, pairs)


PLAN = (
    ("own_behind", "own", 1, 1, ()),
    ("ahead", "own", 0, -1, ()),
    ("behind", "own", 0, 1, ()),
    ("packet", "packet", 0, 1, ()),
    ("over", "ahead", 0, -1, ("ahead",)),
    ("ahead_behind", "ahead", 1, 1, ()),
    ("ahead_ahead", "ahead", 1, -1, ("own_behind",)),
    ("behind_behind", "behind", 1, 1, ("behind",)),
    ("behind_ahead", "behind", 1, -1, ("packet",)),
    ("own_over", "own_behind", 1, 1, ("over",)),
    ("over_behind", "over", 1, 1, ("ahead_behind",)),
    ("over_ahead", "over", 1, -1, ("ahead_ahead",)),
    ("ahead_over", "ahead_behind", 1, 1, ("behind_behind",)),
    ("over_over", "over_ahead", 1, -1, ("over_ahead",)),
    ("own_ahead", "own", 1, -1, ("behind_ahead",)),
    ("behind_over", "behind_behind", 1, 1, ("own_over",)),
)
LAST = ("ahead_over", "over_over", "own_ahead", "behind_over",)
ALONG = {"own": 0, "ahead": 1, "over": 2, "behind": 3}
ACROSS = {"": 0, "_ahead": 1, "_over": 2, "_behind": 3}


def spread(block, packet):
    held = {"own": block}
    for name, source, axis, step, waits in PLAN:
        value = packet if name == "packet" else held[source]
        if waits:
            value = lax.optimization_barrier((value, *[held[w] for w in waits]))[0]
        if name == "packet":
            held[name] = lax.ppermute(value, "ints", [(0, 1), (1, 0)])
        else:
            held[name] = move(value, axis, step)
    packet = held.pop("packet")
    return held, packet


def slot_of(name):
    first, _, second = name.partition("_")
    return ACROSS["_" + second if second else ""] * RING + ALONG[first]


def assemble(copies, base_ref, *refs):
    arrays, table, sems = refs[: len(copies)], refs[-2], refs[-1]
    dmas = []
    for n, slot in enumerate(copies):
        rows = arrays[n].shape[0]
        dmas.append(pltpu.make_async_copy(arrays[n], table.at[pl.ds(base_ref[slot], rows)], sems.at[n]))
    for dma in dmas:
        dma.start()
    for dma in dmas:
        dma.wait()


def kernel(steps, pairs, slots, copies, *refs):
    src_ref, tgt_ref, sign_ref, vb_ref, off_ref, bs_ref, table = refs[:7]
    late = len(copies)
    keep_hbm, give_hbm, g_ref, y_ref, vhi_ref, vlo_ref, acc_ref, sem_out = refs[-8 - bool(late) :][:8]
    dmas = []
    if late:
        base_ref, arrays, table, sems = refs[7], refs[8 : 8 + late], refs[8 + late], refs[-1]
        for n, slot in enumerate(copies):
            rows = arrays[n].shape[0]
            dmas.append(pltpu.make_async_copy(arrays[n], table.at[pl.ds(base_ref[slot], rows)], sems.at[n]))
    for dma in dmas:
        dma.start()
    v = vb_ref[...]
    high = v.astype(jnp.bfloat16)
    vhi_ref[...] = high
    vlo_ref[...] = (v - high.astype(jnp.float32)).astype(jnp.bfloat16)
    acc_ref[...] = jnp.zeros_like(acc_ref)
    for dma in dmas:
        dma.wait()
    rows = GROUP * pairs

    def fetch(step, buffer):
        for r in range(rows):
            g_ref[buffer, r] = table[src_ref[step * rows + r]]

    def mix(step, buffer):
        flat = g_ref.at[buffer].reshape(rows * slots, LANES)
        sign = sign_ref[pl.ds(step, 1), :].astype(jnp.bfloat16)
        left_hi = vhi_ref[...] * sign
        left_lo = vlo_ref[...] * sign
        g = jnp.concatenate([flat[pl.ds(q, rows, stride=slots), :] for q in range(slots)], 1)
        hi = g.astype(jnp.bfloat16)
        lo = (g - hi.astype(jnp.float32)).astype(jnp.bfloat16)
        got = jnp.dot(
            jnp.concatenate([left_hi, left_lo, left_hi], 1),
            jnp.concatenate([hi, hi, lo], 0),
            preferred_element_type=jnp.float32,
        )
        for q in range(slots):
            part = got[:, q * LANES : (q + 1) * LANES]
            y_ref[:, q, pl.ds(step * GROUP, GROUP), :] = part.reshape(pairs, GROUP, LANES)

    fetch(0, 0)

    def some_steps(part, carry):
        for n in range(MIXES):
            step = part * MIXES + n
            fetch(jnp.minimum(step + 1, steps - 1), (n + 1) % 2)
            mix(step, n % 2)
        return carry

    lax.fori_loop(0, steps // MIXES, some_steps, 0)
    lines = lax.broadcasted_iota(jnp.int32, (LANES, LANES), 0)
    tiles = acc_ref.shape[0]

    def place(pair):
        found = []
        for q in range(slots):
            t = tgt_ref[pair * slots + q]
            spot = tgt_ref[(pairs + pair) * slots + q]
            off = off_ref[pl.ds(pair * tiles + t, 1), :]
            sgn = bs_ref[pl.ds(pair * tiles + t, 1), :].astype(jnp.float32)
            hot = jnp.where(lines == off, sgn, 0.0).astype(jnp.bfloat16)
            y = y_ref[pair, q]
            hi = y.astype(jnp.bfloat16)
            lo = (y - hi.astype(jnp.float32)).astype(jnp.bfloat16)
            left = jnp.concatenate([hi, lo], 1)
            right = jnp.concatenate([hot, hot], 0)
            found.append((spot, jnp.dot(left, right, preferred_element_type=jnp.float32)))
        for spot, value in found:
            acc_ref[spot] += value

    def some_pairs(part, carry):
        for n in range(UNROLL):
            place(part * UNROLL + n)
        return carry

    lax.fori_loop(0, pairs // UNROLL, some_pairs, 0)
    half = tiles // 2
    store_give = pltpu.make_async_copy(acc_ref.at[pl.ds(half, half)], give_hbm, sem_out.at[0])
    store_keep = pltpu.make_async_copy(acc_ref.at[pl.ds(0, half)], keep_hbm, sem_out.at[1])
    store_give.start()
    store_keep.start()
    store_give.wait()
    store_keep.wait()


def local(ci_vector, integrals, alpha_source, alpha_sign, beta_tiles, beta_offsets, beta_sign):
    rows_b, cols_a = ci_vector.shape
    pairs, tiles, tile = beta_offsets.shape
    slots = rows_b // tile
    ints = lax.axis_size("ints")
    mine = lax.axis_index("ints")
    cols = cols_a // ints
    alpha = lax.axis_index("alpha")
    x, z = alpha // RING, alpha % RING

    beta = lax.axis_index("beta")
    betas = lax.axis_size("beta")
    rings = betas // CORES
    y, core = beta // CORES, beta % CORES

    columns = ci_vector.T.reshape(cols_a, slots, tile)

    swap = [(0, 1), (1, 0)]
    first = mine == 0
    share = integrals.shape[0]
    both = jnp.stack([alpha_source, alpha_sign]).astype(jnp.float32)
    keep = lax.dynamic_slice_in_dim(both, mine * cols, cols, 2)
    give = lax.dynamic_slice_in_dim(both, (1 - mine) * cols, cols, 2)
    packet = jnp.concatenate([give.reshape(2 * share, cols), jnp.pad(integrals, ((0, 0), (0, cols - pairs)))], 0)
    pieces, packet = spread(columns, packet)
    got = packet[: 2 * share].reshape(2, share, cols)
    v_got = packet[2 * share :, :pairs]
    full = jnp.concatenate([jnp.where(first, keep, got), jnp.where(first, got, keep)], 1)
    v = jnp.concatenate([jnp.where(first, integrals, v_got), jnp.where(first, v_got, integrals)], 0)
    flat = full.transpose(0, 2, 1).reshape(2, cols * pairs)
    source = flat[0].astype(jnp.int32)
    steps = cols // GROUP
    sign = flat[1].reshape(steps, GROUP * pairs)
    eye = jnp.eye(GROUP, dtype=jnp.float32)
    vb = (v.T[:, None, None, :] * eye[None, :, :, None]).reshape(pairs * GROUP, GROUP * pairs)

    wanted = beta * slots + jnp.arange(slots, dtype=jnp.int32)
    hit = beta_tiles[:, :, None] == wanted[None, None, :]
    target = jnp.sum(jnp.where(hit, jnp.arange(tiles, dtype=jnp.int32)[None, :, None], 0), axis=1).reshape(-1)
    owner = target // slots
    away = (owner // CORES - y) % rings
    spot = ((owner % CORES) ^ core) * (tiles // CORES) + away * slots + target % slots
    target = jnp.concatenate([target, spot])

    d = jnp.arange(RING * RING, dtype=jnp.int32)
    dx = jnp.where(core == 0, d // RING, d % RING)
    dz = jnp.where(core == 0, d % RING, d // RING)
    base = (((x + dx) % RING) * RING + (z + dz) % RING) * cols_a

    smem = pl.BlockSpec(memory_space=pltpu.SMEM)
    vmem = pl.BlockSpec(memory_space=pltpu.VMEM)
    hbm = pl.BlockSpec(memory_space=pl.ANY)
    whole = jax.ShapeDtypeStruct((lax.axis_size("alpha") * cols_a, slots, tile), jnp.float32)
    early = tuple(n for n in pieces if n not in LAST)
    table = pl.pallas_call(
        functools.partial(assemble, tuple(slot_of(n) for n in early)),
        out_shape=whole,
        in_specs=[smem] + [hbm] * len(early),
        out_specs=vmem,
        scratch_shapes=[pltpu.SemaphoreType.DMA((len(early),))],
        compiler_params=pltpu.CompilerParams(vmem_limit_bytes=12 * 1024 * 1024),
        name="assemble",
    )(base, *[pieces[n] for n in early])
    width = cols // CHUNKS
    offsets = beta_offsets.reshape(pairs * tiles, tile)
    signs = beta_sign.reshape(pairs * tiles, tile)
    across = [(b, b ^ 1) for b in range(betas)]
    half = jax.ShapeDtypeStruct((tiles // CORES, width, tile), jnp.float32)
    part_steps = steps // CHUNKS
    sums = []
    for chunk in range(CHUNKS):
        late = LAST if chunk == 0 else ()
        outs = pl.pallas_call(
            functools.partial(kernel, part_steps, pairs, slots, tuple(slot_of(n) for n in late)),
            out_shape=((whole,) if late else ()) + (half, half),
            in_specs=[smem] * 2 + [vmem] * 5 + [smem] * bool(late) + [hbm] * len(late),
            out_specs=((vmem,) if late else ()) + (hbm, hbm),
            scratch_shapes=[
                pltpu.VMEM((2, GROUP * pairs, slots, tile), jnp.float32),
                pltpu.VMEM((pairs, slots, width, tile), jnp.float32),
                pltpu.VMEM((GROUP * pairs, GROUP * pairs), jnp.bfloat16),
                pltpu.VMEM((GROUP * pairs, GROUP * pairs), jnp.bfloat16),
                pltpu.VMEM((tiles, width, tile), jnp.float32),
                pltpu.SemaphoreType.DMA((2,)),
            ]
            + [pltpu.SemaphoreType.DMA((len(late),))] * bool(late),
            input_output_aliases={6: 0} if late else {},
            compiler_params=pltpu.CompilerParams(vmem_limit_bytes=12 * 1024 * 1024),
            cost_estimate=pl.CostEstimate(flops=4 * 10**9, bytes_accessed=2**23, transcendentals=0),
            name="sigma_partial",
        )(
            lax.slice_in_dim(source, chunk * width * pairs, (chunk + 1) * width * pairs),
            target,
            lax.slice_in_dim(sign, chunk * part_steps, (chunk + 1) * part_steps),
            vb,
            offsets,
            signs,
            table,
            *([base] * bool(late)),
            *[pieces[n] for n in late],
        )
        if late:
            table, keep, give = outs
        else:
            keep, give = outs
        came = lax.ppermute(give, "beta", across)
        total = keep[:slots] + came[:slots]
        for far in (2, 1, 3):
            pairs_y = [(b, (b + far * CORES) % betas) for b in range(betas)]
            part = keep[far * slots : (far + 1) * slots] + came[far * slots : (far + 1) * slots]
            total = total + lax.ppermute(part, "beta", pairs_y)
        sums.append((total, lax.ppermute(total, "ints", swap)))
    mine_all = jnp.concatenate([m for m, _ in sums], 1)
    other_all = jnp.concatenate([o for _, o in sums], 1)
    joined = jnp.concatenate([jnp.where(first, mine_all, other_all), jnp.where(first, other_all, mine_all)], 1)
    return joined.transpose(0, 2, 1).reshape(rows_b, cols_a)


def solution(mesh):
    return jax.shard_map(
        local,
        mesh=mesh,
        in_specs=(
            P("beta", "alpha"),
            P("ints", None),
            P("ints", "alpha"),
            P("ints", "alpha"),
            P(),
            P(),
            P(),
        ),
        out_specs=P("beta", "alpha"),
        check_vma=False,
    )
```

```python
import functools

import jax
import jax.numpy as jnp
from jax import lax
from jax.experimental import pallas as pl
from jax.experimental.pallas import tpu as pltpu
from jax.sharding import PartitionSpec as P

LANES = 128
GROUP = 8
RING = 4
CORES = 2
CHUNKS = 2
UNROLL = 32
MIXES = 8
FLIGHT = 5
AXES = ("alpha", "beta", "ints")


def device(x, z, y, core):
    ints = lax.axis_size("ints")
    x, z = x % RING, z % (RING * ints)
    alpha = x * RING + z % RING
    return (alpha * lax.axis_size("beta") + y * CORES + core) * ints + z // RING


def move(value, axis, step):
    pairs = []
    for x in range(lax.axis_size("alpha") // RING):
        for z in range(RING * lax.axis_size("ints")):
            for y in range(lax.axis_size("beta") // CORES):
                for core in range(CORES):
                    dx, dz = (step, 0) if axis != core else (0, step)
                    pairs.append((device(x, z, y, core), device(x + dx, z + dz, y, core)))
    return lax.ppermute(value, AXES, pairs)


PLAN = (
    ("own_behind", "own", 1, 1, ()),
    ("ahead", "own", 0, -1, ()),
    ("behind", "own", 0, 1, ()),
    ("packet", "packet", 0, 1, ()),
    ("over", "ahead", 0, -1, ("ahead",)),
    ("ahead_behind", "ahead", 1, 1, ()),
    ("ahead_ahead", "ahead", 1, -1, ("own_behind",)),
    ("behind_behind", "behind", 1, 1, ("behind",)),
    ("behind_ahead", "behind", 1, -1, ("packet",)),
    ("own_over", "own_behind", 1, 1, ("over",)),
    ("over_behind", "over", 1, 1, ("ahead_behind",)),
    ("over_ahead", "over", 1, -1, ("ahead_ahead",)),
    ("ahead_over", "ahead_behind", 1, 1, ("behind_behind",)),
    ("over_over", "over_ahead", 1, -1, ("over_ahead",)),
    ("own_ahead", "own", 1, -1, ("behind_ahead",)),
    ("behind_over", "behind_behind", 1, 1, ("own_over",)),
)
LAST = ("ahead_over", "over_over", "own_ahead", "behind_over",)
ALONG = {"own": 0, "ahead": 1, "over": 2, "behind": 3}
ACROSS = {"": 0, "_ahead": 1, "_over": 2, "_behind": 3}


def spread(block, packet):
    held = {"own": block}
    for name, source, axis, step, waits in PLAN:
        value = packet if name == "packet" else held[source]
        if waits:
            value = lax.optimization_barrier((value, *[held[w] for w in waits]))[0]
        if name == "packet":
            held[name] = lax.ppermute(value, "ints", [(0, 1), (1, 0)])
        else:
            held[name] = move(value, axis, step)
    packet = held.pop("packet")
    return held, packet


def slot_of(name):
    first, _, second = name.partition("_")
    return ACROSS["_" + second if second else ""] * RING + ALONG[first]


def assemble(copies, base_ref, *refs):
    arrays, table, sems = refs[: len(copies)], refs[-2], refs[-1]
    dmas = []
    for n, slot in enumerate(copies):
        rows = arrays[n].shape[0]
        dmas.append(pltpu.make_async_copy(arrays[n], table.at[pl.ds(base_ref[slot], rows)], sems.at[n]))
    for dma in dmas:
        dma.start()
    for dma in dmas:
        dma.wait()


def kernel(steps, pairs, slots, copies, *refs):
    src_ref, tgt_ref, sign_ref, vb_ref, off_ref, bs_ref, table = refs[:7]
    late = len(copies)
    keep_hbm, give_hbm, g_ref, y_ref, vhi_ref, vlo_ref, acc_ref, sem_out = refs[-8 - bool(late) :][:8]
    dmas = []
    if late:
        base_ref, arrays, table, sems = refs[7], refs[8 : 8 + late], refs[8 + late], refs[-1]
        for n, slot in enumerate(copies):
            rows = arrays[n].shape[0]
            dmas.append(pltpu.make_async_copy(arrays[n], table.at[pl.ds(base_ref[slot], rows)], sems.at[n]))
    for dma in dmas:
        dma.start()
    v = vb_ref[...]
    high = v.astype(jnp.bfloat16)
    vhi_ref[...] = high
    vlo_ref[...] = (v - high.astype(jnp.float32)).astype(jnp.bfloat16)
    acc_ref[...] = jnp.zeros_like(acc_ref)
    for dma in dmas:
        dma.wait()
    rows = GROUP * pairs

    def fetch(step, buffer):
        for r in range(rows):
            g_ref[buffer, r] = table[src_ref[step * rows + r]]

    def mix(step, buffer):
        flat = g_ref.at[buffer].reshape(rows * slots, LANES)
        sign = sign_ref[pl.ds(step, 1), :].astype(jnp.bfloat16)
        left_hi = vhi_ref[...] * sign
        left_lo = vlo_ref[...] * sign
        g = jnp.concatenate([flat[pl.ds(q, rows, stride=slots), :] for q in range(slots)], 1)
        hi = g.astype(jnp.bfloat16)
        lo = (g - hi.astype(jnp.float32)).astype(jnp.bfloat16)
        got = jnp.dot(
            jnp.concatenate([left_hi, left_lo, left_hi], 1),
            jnp.concatenate([hi, hi, lo], 0),
            preferred_element_type=jnp.float32,
        )
        for q in range(slots):
            part = got[:, q * LANES : (q + 1) * LANES]
            y_ref[:, q, pl.ds(step * GROUP, GROUP), :] = part.reshape(pairs, GROUP, LANES)

    fetch(0, 0)

    def some_steps(part, carry):
        for n in range(MIXES):
            step = part * MIXES + n
            fetch(jnp.minimum(step + 1, steps - 1), (n + 1) % 2)
            mix(step, n % 2)
        return carry

    lax.fori_loop(0, steps // MIXES, some_steps, 0)
    lines = lax.broadcasted_iota(jnp.int32, (LANES, LANES), 0)
    tiles = acc_ref.shape[0]

    def place(pair):
        found = []
        for q in range(slots):
            t = tgt_ref[pair * slots + q]
            spot = tgt_ref[(pairs + pair) * slots + q]
            off = off_ref[pl.ds(pair * tiles + t, 1), :]
            sgn = bs_ref[pl.ds(pair * tiles + t, 1), :].astype(jnp.float32)
            hot = jnp.where(lines == off, sgn, 0.0).astype(jnp.bfloat16)
            y = y_ref[pair, q]
            hi = y.astype(jnp.bfloat16)
            lo = (y - hi.astype(jnp.float32)).astype(jnp.bfloat16)
            left = jnp.concatenate([hi, lo], 1)
            right = jnp.concatenate([hot, hot], 0)
            found.append((spot, jnp.dot(left, right, preferred_element_type=jnp.float32)))
        for spot, value in found:
            acc_ref[spot] += value

    def some_pairs(part, carry):
        for n in range(UNROLL):
            place(part * UNROLL + n)
        return carry

    lax.fori_loop(0, pairs // UNROLL, some_pairs, 0)
    half = tiles // 2
    store_give = pltpu.make_async_copy(acc_ref.at[pl.ds(half, half)], give_hbm, sem_out.at[0])
    store_keep = pltpu.make_async_copy(acc_ref.at[pl.ds(0, half)], keep_hbm, sem_out.at[1])
    store_give.start()
    store_keep.start()
    store_give.wait()
    store_keep.wait()


def local(ci_vector, integrals, alpha_source, alpha_sign, beta_tiles, beta_offsets, beta_sign):
    rows_b, cols_a = ci_vector.shape
    pairs, tiles, tile = beta_offsets.shape
    slots = rows_b // tile
    ints = lax.axis_size("ints")
    mine = lax.axis_index("ints")
    cols = cols_a // ints
    alpha = lax.axis_index("alpha")
    x, z = alpha // RING, alpha % RING

    beta = lax.axis_index("beta")
    betas = lax.axis_size("beta")
    rings = betas // CORES
    y, core = beta // CORES, beta % CORES

    columns = ci_vector.T.reshape(cols_a, slots, tile)

    swap = [(0, 1), (1, 0)]
    first = mine == 0
    share = integrals.shape[0]
    both = jnp.stack([alpha_source, alpha_sign]).astype(jnp.float32)
    keep = lax.dynamic_slice_in_dim(both, mine * cols, cols, 2)
    give = lax.dynamic_slice_in_dim(both, (1 - mine) * cols, cols, 2)
    packet = jnp.concatenate([give.reshape(2 * share, cols), jnp.pad(integrals, ((0, 0), (0, cols - pairs)))], 0)
    pieces, packet = spread(columns, packet)
    got = packet[: 2 * share].reshape(2, share, cols)
    v_got = packet[2 * share :, :pairs]
    full = jnp.concatenate([jnp.where(first, keep, got), jnp.where(first, got, keep)], 1)
    v = jnp.concatenate([jnp.where(first, integrals, v_got), jnp.where(first, v_got, integrals)], 0)
    flat = full.transpose(0, 2, 1).reshape(2, cols * pairs)
    source = flat[0].astype(jnp.int32)
    steps = cols // GROUP
    sign = flat[1].reshape(steps, GROUP * pairs)
    eye = jnp.eye(GROUP, dtype=jnp.float32)
    vb = (v.T[:, None, None, :] * eye[None, :, :, None]).reshape(pairs * GROUP, GROUP * pairs)

    wanted = beta * slots + jnp.arange(slots, dtype=jnp.int32)
    hit = beta_tiles[:, :, None] == wanted[None, None, :]
    target = jnp.sum(jnp.where(hit, jnp.arange(tiles, dtype=jnp.int32)[None, :, None], 0), axis=1).reshape(-1)
    owner = target // slots
    away = (owner // CORES - y) % rings
    spot = ((owner % CORES) ^ core) * (tiles // CORES) + away * slots + target % slots
    target = jnp.concatenate([target, spot])

    d = jnp.arange(RING * RING, dtype=jnp.int32)
    dx = jnp.where(core == 0, d // RING, d % RING)
    dz = jnp.where(core == 0, d % RING, d // RING)
    base = (((x + dx) % RING) * RING + (z + dz) % RING) * cols_a

    smem = pl.BlockSpec(memory_space=pltpu.SMEM)
    vmem = pl.BlockSpec(memory_space=pltpu.VMEM)
    hbm = pl.BlockSpec(memory_space=pl.ANY)
    whole = jax.ShapeDtypeStruct((lax.axis_size("alpha") * cols_a, slots, tile), jnp.float32)
    early = tuple(n for n in pieces if n not in LAST)
    table = pl.pallas_call(
        functools.partial(assemble, tuple(slot_of(n) for n in early)),
        out_shape=whole,
        in_specs=[smem] + [hbm] * len(early),
        out_specs=vmem,
        scratch_shapes=[pltpu.SemaphoreType.DMA((len(early),))],
        compiler_params=pltpu.CompilerParams(vmem_limit_bytes=12 * 1024 * 1024),
        name="assemble",
    )(base, *[pieces[n] for n in early])
    width = cols // CHUNKS
    offsets = beta_offsets.reshape(pairs * tiles, tile)
    signs = beta_sign.reshape(pairs * tiles, tile)
    across = [(b, b ^ 1) for b in range(betas)]
    half = jax.ShapeDtypeStruct((tiles // CORES, width, tile), jnp.float32)
    part_steps = steps // CHUNKS
    sums = []
    for chunk in range(CHUNKS):
        late = LAST if chunk == 0 else ()
        outs = pl.pallas_call(
            functools.partial(kernel, part_steps, pairs, slots, tuple(slot_of(n) for n in late)),
            out_shape=((whole,) if late else ()) + (half, half),
            in_specs=[smem] * 2 + [vmem] * 5 + [smem] * bool(late) + [hbm] * len(late),
            out_specs=((vmem,) if late else ()) + (hbm, hbm),
            scratch_shapes=[
                pltpu.VMEM((2, GROUP * pairs, slots, tile), jnp.float32),
                pltpu.VMEM((pairs, slots, width, tile), jnp.float32),
                pltpu.VMEM((GROUP * pairs, GROUP * pairs), jnp.bfloat16),
                pltpu.VMEM((GROUP * pairs, GROUP * pairs), jnp.bfloat16),
                pltpu.VMEM((tiles, width, tile), jnp.float32),
                pltpu.SemaphoreType.DMA((2,)),
            ]
            + [pltpu.SemaphoreType.DMA((len(late),))] * bool(late),
            input_output_aliases={6: 0} if late else {},
            compiler_params=pltpu.CompilerParams(vmem_limit_bytes=12 * 1024 * 1024),
            cost_estimate=pl.CostEstimate(flops=4 * 10**9, bytes_accessed=2**23, transcendentals=0),
            name="sigma_partial",
        )(
            lax.slice_in_dim(source, chunk * width * pairs, (chunk + 1) * width * pairs),
            target,
            lax.slice_in_dim(sign, chunk * part_steps, (chunk + 1) * part_steps),
            vb,
            offsets,
            signs,
            table,
            *([base] * bool(late)),
            *[pieces[n] for n in late],
        )
        if late:
            table, keep, give = outs
        else:
            keep, give = outs
        came = lax.ppermute(give, "beta", across)
        total = keep[:slots] + came[:slots]
        for far in (2, 1, 3):
            pairs_y = [(b, (b + far * CORES) % betas) for b in range(betas)]
            part = keep[far * slots : (far + 1) * slots] + came[far * slots : (far + 1) * slots]
            total = total + lax.ppermute(part, "beta", pairs_y)
        sums.append((total, lax.ppermute(total, "ints", swap)))
    mine_all = jnp.concatenate([m for m, _ in sums], 1).transpose(0, 2, 1).reshape(rows_b, cols)
    other_all = jnp.concatenate([o for _, o in sums], 1).transpose(0, 2, 1).reshape(rows_b, cols)
    return jnp.concatenate([jnp.where(first, mine_all, other_all), jnp.where(first, other_all, mine_all)], 1)


def solution(mesh):
    return jax.shard_map(
        local,
        mesh=mesh,
        in_specs=(
            P("beta", "alpha"),
            P("ints", None),
            P("ints", "alpha"),
            P("ints", "alpha"),
            P(),
            P(),
            P(),
        ),
        out_specs=P("beta", "alpha"),
        check_vma=False,
    )
```
